256 devices in a mesh: dp: 4 (over y_lo, core), depth: 32 (over x, z), height: 2 (over y_hi).
Axes of the slice: x: 4, y: 4 (y_hi: 2, y_lo: 2; y = y_hi * 2 + y_lo), z: 8, core: 2. Of those that a mesh axis runs over, the one named last changes fastest.
Arguments:
- activations: bfloat16 [4, 128, 32, 64, 128], P('dp', 'depth', 'height'), may hold values from -6 to 6
- error_signal: bfloat16 [4, 128, 32, 64, 128], P('dp', 'depth', 'height'), may hold values from -6 to 6
- kernel: bfloat16 [3, 3, 3, 128, 128], replicated, may hold values from -0.109375 to 0.109375
Outputs:
- input_grad: bfloat16 [4, 128, 32, 64, 128], P('dp', 'depth', 'height')
- kernel_grad: float32 [3, 3, 3, 128, 128], replicated
The draws below stay inside these ranges and needn't reach their ends.
All inputs are finite; a program needn't handle non-finite values.
Results may differ from the reference program's by a relative error of at most 0.0011.
Values may be sent and summed in bfloat16 or wider, within the bound.
A program may use at most 128 MiB of HBM per device.

```python
import jax
import jax.numpy as jnp
from jax import lax

C = 128
CW = 64
BATCH = 4
NDEPTH = 128
NHEIGHT = 32


def steps_of(key, shape, shards, smallest, high):
    level = 1.0
    for dim, parts in shards:
        heights = jax.random.uniform(jax.random.fold_in(jax.random.fold_in(key, 6), dim), (parts,), jnp.float32, smallest / len(shards), high / len(shards))
        level = level * jnp.repeat(jnp.exp(heights), shape[dim] // parts).reshape((-1,) + (1,) * (len(shape) - 1 - dim))
    return level


def gaussian(key, extent, scale, limit, shards=(), kind=jnp.bfloat16):
    level = steps_of(key, extent, shards, -0.22, 0.18) if shards else 1.0
    result = jax.random.normal(key, extent, jnp.float32) * scale * level
    return jnp.minimum(jnp.maximum(result, -limit), limit).astype(kind)


def setup_inputs(seed: int = 0) -> dict:
    splits = jax.random.split(jax.random.key(seed), 4)
    activations = gaussian(splits[0], (BATCH, NDEPTH, NHEIGHT, CW, C), 1.0, 6.0, ((0, 4), (1, 32), (2, 2)))
    error_signal = gaussian(splits[1], (BATCH, NDEPTH, NHEIGHT, CW, C), 1.0, 6.0, ((0, 4), (1, 32), (2, 2)))
    kernel = gaussian(splits[2], (3, 3, 3, C, C), (27 * C) ** -0.5, 0.109375)
    return {"activations": activations, "error_signal": error_signal, "kernel": kernel}


def one_sample(pair, kernel):
    inputs, errors = pair
    padded = jnp.pad(errors, ((1, 1), (1, 1), (1, 1), (0, 0)))
    depth_len, height_len, width_len, chans = inputs.shape
    flat_in = inputs.reshape(-1, chans)
    grad_in = jnp.zeros((depth_len * height_len * width_len, chans), jnp.float32)
    tap_grads = []
    for tap_a in range(3):
        for tap_h in range(3):
            for tap_w in range(3):
                shifted = padded[2 - tap_a:2 - tap_a + depth_len, 2 - tap_h:2 - tap_h + height_len, 2 - tap_w:2 - tap_w + width_len]
                shifted = shifted.reshape(-1, chans)
                grad_in = grad_in + jnp.dot(shifted, kernel[tap_a, tap_h, tap_w].T, preferred_element_type=jnp.float32)
                tap_grads.append(jnp.dot(flat_in.T, shifted, preferred_element_type=jnp.float32))
    grad_in = grad_in.reshape(inputs.shape).astype(jnp.bfloat16)
    return (grad_in, jnp.stack(tap_grads).reshape(3, 3, 3, chans, chans))

def reference(activations, error_signal, kernel):
    input_grad, per_sample = lax.map(lambda pair: one_sample(pair, kernel), (activations, error_signal))
    scale_factor = 1.0 / jnp.sqrt(jnp.float32(BATCH * NDEPTH * NHEIGHT * CW))
    kernel_grad = lax.optimization_barrier(jnp.sum(per_sample, axis=0)) * scale_factor
    return (input_grad, kernel_grad)
```

```python
import functools

import jax
import jax.numpy as jnp
from jax import lax
from jax.experimental import pallas as pl
from jax.experimental.pallas import tpu as pltpu
from jax.sharding import PartitionSpec as P

MESH = pl.DeviceIdType.MESH
F32 = jnp.float32
BF16 = jnp.bfloat16
NX, NY, NZ = 4, 4, 8
CHUNKS = (((1,), 5), ((0, 2), 9))


def device_of(core, x, y, z):
    return ((y % 2) * 2 + core, x * NZ + z, y // 2)


def body(
    act_hbm, err_hbm, ker_hbm, ig_hbm, kg_hbm,
    raw, act_v, ker_v, e3, at, wm, fs, ig_v, gs, hs, r1s, r2s, r3s, fins,
    lsem, osem, hsend, hrecv, s1s, s1r, s2s, s2r, s3s, s3r, s4s, s4r, s5s, s5r,
):
    dp = lax.axis_index("dp")
    dep = lax.axis_index("depth")
    he = lax.axis_index("height")
    core = dp % 2
    y = he * 2 + dp // 2
    x = dep // NZ
    z = dep % NZ
    me = y * NX + x
    n_dep = NX * NZ
    up = (dp, (dep + 1) % n_dep, he)
    down = (dp, (dep + n_dep - 1) % n_dep, he)
    side = (dp, dep, 1 - he)
    up_side = (dp, (dep + 1) % n_dep, 1 - he)
    down_side = (dp, (dep + n_dep - 1) % n_dep, 1 - he)
    sibling = device_of(1 - core, x, y, z)
    plane = []
    for j in (10, 6, 14, 9, 11, 5, 7, 13, 15, 2, 8, 1, 3, 4, 12):
        px, py = (x + j % NX) % NX, (y + j // NX) % NY
        plane.append((py * NX + px, device_of(core, px, py, z)))
    line = []
    for j in (4, 3, 5, 2, 6, 1, 7):
        pz = (z + j) % NZ
        line.append((pz, device_of(core, x, y, pz)))

    barrier = pltpu.get_barrier_semaphore()
    others = [up, down, side, up_side, down_side, sibling]
    others += [d for _, d in plane] + [d for _, d in line]

    load_err = pltpu.make_async_copy(err_hbm.at[0], raw.at[1:5, 1:17], lsem.at[0])
    load_act = pltpu.make_async_copy(act_hbm.at[0], act_v, lsem.at[1])
    load_ker = pltpu.make_async_copy(ker_hbm, ker_v, lsem.at[2])
    load_err.start()
    load_act.start()
    load_ker.start()
    for d in others:
        pl.semaphore_signal(barrier, inc=1, device_id=d, device_id_type=MESH)

    for s in range(6):
        raw[s, he * 17] = jnp.zeros((64, 128), BF16)
    fs[:, 0:8] = jnp.zeros((18, 8, 128), F32)
    fs[:, 72:80] = jnp.zeros((18, 8, 128), F32)
    for g, (slabs, n) in zip(gs, CHUNKS):
        used = len(slabs) * 72
        if used < 16 * n:
            g[:, used:] = jnp.zeros((2, 16 * n - used, 8, 128), F32)

    load_act.wait()

    @pl.loop(0, 4)
    def _(d):
        at[d] = act_v[d].reshape(1024, 128).T

    pl.semaphore_wait(barrier, len(others))

    row_src = 15 - 15 * he
    row_dst = 17 * he

    def remote(src, dst, send, recv, target):
        return pltpu.make_async_remote_copy(
            src_ref=src, dst_ref=dst, send_sem=send, recv_sem=recv,
            device_id=target, device_id_type=MESH,
        )

    halo = [
        remote(err_hbm.at[0, :, row_src], raw.at[1:5, row_dst], hsend.at[0], hrecv.at[0], side),
        remote(err_hbm.at[0, 3], raw.at[0, 1:17], hsend.at[1], hrecv.at[1], up),
        remote(err_hbm.at[0, 0], raw.at[5, 1:17], hsend.at[2], hrecv.at[2], down),
        remote(err_hbm.at[0, 3, row_src], raw.at[0, row_dst], hsend.at[3], hrecv.at[3], up_side),
        remote(err_hbm.at[0, 0, row_src], raw.at[5, row_dst], hsend.at[4], hrecv.at[4], down_side),
    ]
    for c in halo:
        c.start()

    load_ker.wait()

    @pl.loop(0, 3)
    def _(a):
        for r in range(4):
            for e in range(2):
                tap = e + 2 - r
                for j in range(3):
                    if 0 <= tap <= 2:
                        block = ker_v[a * 9 + tap * 3 + 2 - j].T
                    else:
                        block = jnp.zeros((128, 128), BF16)
                    wm[a * 4 + r, j * 128 : (j + 1) * 128, e * 128 : (e + 1) * 128] = block

    def widen(s):
        fs[:, 8:72] = raw[s].astype(F32)
        e3[s, :, :, 0:128] = fs[:, 7:71].astype(BF16)
        e3[s, :, :, 128:256] = raw[s]
        e3[s, :, :, 256:384] = fs[:, 9:73].astype(BF16)

    load_err.wait()
    halo[0].wait()

    @pl.loop(1, 5)
    def _(s):
        widen(s)

    def grad_terms(a, pairs, h):
        total = None
        for d, s in pairs:
            term = jnp.dot(
                at[d], e3[s, 2 - h : 18 - h].reshape(1024, 384), preferred_element_type=F32
            )
            total = term if total is None else total + term
        return total

    def put(ch, first, h, total, add):
        g = gs[ch]
        for j in range(3):
            for c in range(2):
                place = (c, pl.ds(first + (h * 3 + 2 - j) * 8, 8))
                part = total[c * 64 : (c + 1) * 64, j * 128 : (j + 1) * 128].reshape(8, 8, 128)
                if add:
                    part = part + g[place]
                g[place] = part

    def s1(ch):
        return remote(gs[ch].at[1 - core], r1s[ch], s1s.at[ch], s1r.at[ch], sibling)

    def s2(ch):
        n = CHUNKS[ch][1]
        return [
            remote(hs[ch].at[pl.ds(p * n, n)], r2s[ch].at[me], s2s.at[ch, p], s2r.at[ch, me], d)
            for p, d in plane
        ]

    def s2_arrive(ch):
        n = CHUNKS[ch][1]
        for p, d in plane:
            remote(
                hs[ch].at[pl.ds(p * n, n)], r2s[ch].at[p], s2s.at[ch, p], s2r.at[ch, p], d
            ).wait()

    def s3(ch):
        return [
            remote(r3s[ch].at[z], r3s[ch].at[z], s3s.at[ch, p], s3r.at[ch, z], d) for p, d in line
        ]

    def s4_part(ch, p):
        n = CHUNKS[ch][1]
        return fins[ch].at[core, pl.ds(p * n, n)]

    def s4(ch):
        return [
            remote(s4_part(ch, me), s4_part(ch, me), s4s.at[ch, p], s4r.at[ch, me], d)
            for p, d in plane
        ]

    def s5(ch):
        return remote(fins[ch].at[core], fins[ch].at[core], s5s.at[ch], s5r.at[ch], sibling)

    def step1(ch):
        s1(ch).start()

    def step2(ch):
        s1(ch).wait()
        hs[ch][...] = gs[ch][core] + r1s[ch][...]
        for c in s2(ch):
            c.start()

    def step3(ch):
        n = CHUNKS[ch][1]
        s2_arrive(ch)
        r2s[ch][me] = hs[ch][pl.ds(me * n, n)]
        total = r2s[ch][0]
        for p in range(1, 16):
            total = total + r2s[ch][p]
        r3s[ch][z] = total
        for c in s3(ch):
            c.start()

    def step4(ch):
        n = CHUNKS[ch][1]
        for p, d in line:
            remote(r3s[ch].at[z], r3s[ch].at[p], s3s.at[ch, p], s3r.at[ch, p], d).wait()
        total = r3s[ch][0]
        for p in range(1, NZ):
            total = total + r3s[ch][p]
        fins[ch][core, pl.ds(me * n, n)] = total * (1.0 / 1024.0)
        for c in s4(ch):
            c.start()

    def step5(ch):
        for p, d in plane:
            remote(s4_part(ch, me), s4_part(ch, p), s4s.at[ch, p], s4r.at[ch, p], d).wait()
        s5(ch).start()

    def outs(ch):
        slabs, n = CHUNKS[ch]
        copies = []
        for i, a in enumerate(slabs):
            for c in range(2):
                copies.append(
                    pltpu.make_async_copy(
                        fins[ch].at[c, i * 72 : (i + 1) * 72],
                        kg_hbm.at[c, a * 72 : (a + 1) * 72],
                        osem.at[a * 2 + c],
                    )
                )
        return copies

    def step6(ch):
        remote(fins[ch].at[core], fins[ch].at[1 - core], s5s.at[ch], s5r.at[ch], sibling).wait()
        for c in outs(ch):
            c.start()

    for h in range(3):
        put(0, 0, h, grad_terms(1, [(d, d + 1) for d in range(4)], h), False)
    step1(0)

    @pl.loop(0, 2)
    def _(i):
        for h in range(3):
            total = grad_terms(2 * i, [(d + i, d + 2 - i) for d in range(3)], h)
            put(1, i * 72, h, total, False)

        @pl.when(i == 0)
        def _():
            step2(0)

    for c in halo[1:]:
        c.wait()

    @pl.when(dep == 0)
    def _():
        raw[0] = jnp.zeros((18, 64, 128), BF16)

    @pl.when(dep == n_dep - 1)
    def _():
        raw[5] = jnp.zeros((18, 64, 128), BF16)

    @pl.loop(0, 2)
    def _(i):
        widen(5 - 5 * i)
        for h in range(3):
            put(1, i * 72, h, grad_terms(2 * i, [(3 - 3 * i, 5 - 5 * i)], h), True)

    step1(1)
    step3(0)

    @pl.loop(0, 4)
    def _(d):
        acc = jnp.zeros((512, 256), F32)
        for a in range(3):
            rows = e3.at[d + 2 - a]
            for r in range(4):
                part = rows[...].reshape(9, 2, 64, 384)[r // 2 : r // 2 + 8, r % 2]
                acc += jnp.dot(part.reshape(512, 384), wm[a * 4 + r], preferred_element_type=F32)
        for e in range(2):
            half = acc[:, e * 128 : (e + 1) * 128].astype(BF16).reshape(8, 64, 128)
            for k in range(8):
                ig_v[d, 2 * k + e] = half[k]

        @pl.when(d == 0)
        def _():
            step2(1)
            step4(0)

        @pl.when(d == 2)
        def _():
            step3(1)
            step5(0)

    store = pltpu.make_async_copy(ig_v, ig_hbm.at[0], osem.at[6])
    store.start()
    step4(1)
    step6(0)
    step5(1)
    step6(1)
    for ch in range(len(CHUNKS)):
        for c in outs(ch):
            c.wait()
    store.wait()


def local(activations, error_signal, kernel):
    any_spec = pl.BlockSpec(memory_space=pl.ANY)
    tiles = [n for _, n in CHUNKS]
    count = len(CHUNKS)

    def per_chunk(shape):
        return [pltpu.VMEM(shape(n) + (8, 128), F32) for n in tiles]

    dma = pltpu.SemaphoreType.DMA
    input_grad, packed = pl.pallas_call(
        body,
        out_shape=(
            jax.ShapeDtypeStruct(activations.shape, BF16),
            jax.ShapeDtypeStruct((2, 216, 8, 128), F32),
        ),
        in_specs=[any_spec] * 3,
        out_specs=(any_spec, any_spec),
        scratch_shapes=[
            pltpu.VMEM((6, 18, 64, 128), BF16),
            pltpu.VMEM((4, 16, 64, 128), BF16),
            pltpu.VMEM((27, 128, 128), BF16),
            pltpu.VMEM((6, 18, 64, 384), BF16),
            pltpu.VMEM((4, 128, 1024), BF16),
            pltpu.VMEM((12, 384, 256), BF16),
            pltpu.VMEM((18, 80, 128), F32),
            pltpu.VMEM((4, 16, 64, 128), BF16),
            per_chunk(lambda n: (2, 16 * n)),
            per_chunk(lambda n: (16 * n,)),
            per_chunk(lambda n: (16 * n,)),
            per_chunk(lambda n: (16, n)),
            per_chunk(lambda n: (NZ, n)),
            per_chunk(lambda n: (2, 16 * n)),
            dma((3,)),
            dma((7,)),
            dma((5,)),
            dma((5,)),
            dma((count,)),
            dma((count,)),
            dma((count, 16)),
            dma((count, 16)),
            dma((count, NZ)),
            dma((count, NZ)),
            dma((count, 16)),
            dma((count, 16)),
            dma((count,)),
            dma((count,)),
        ],
        compiler_params=pltpu.CompilerParams(
            collective_id=0, has_side_effects=True, vmem_limit_bytes=48 << 20
        ),
        cost_estimate=pl.CostEstimate(flops=8 << 30, bytes_accessed=6 << 20, transcendentals=0),
        name="conv_grads",
    )(activations, error_signal, kernel.reshape(27, 128, 128))
    taps = jnp.transpose(packed.reshape(2, 27, 64, 128), (1, 0, 2, 3))
    return (input_grad, taps.reshape(3, 3, 3, 128, 128))


def solution(mesh):
    placed = P("dp", "depth", "height", None, None)
    return jax.shard_map(
        local,
        mesh=mesh,
        in_specs=(placed, placed, P()),
        out_specs=(placed, P()),
        check_vma=False,
    )
```

```python
import functools

import jax
import jax.numpy as jnp
from jax import lax
from jax.experimental import pallas as pl
from jax.experimental.pallas import tpu as pltpu
from jax.sharding import PartitionSpec as P

MESH = pl.DeviceIdType.MESH
F32 = jnp.float32
BF16 = jnp.bfloat16
NX, NY, NZ = 4, 4, 8
CHUNKS = (
    (((1, 0), (1, 1), (1, 2)), 5),
    (((0, 0), (0, 1), (0, 2), (2, 0)), 6),
    (((2, 1), (2, 2)), 3),
)
PLACE = {row: (ch, 24 * i) for ch, (rows, _) in enumerate(CHUNKS) for i, row in enumerate(rows)}


def device_of(core, x, y, z):
    return ((y % 2) * 2 + core, x * NZ + z, y // 2)


def body(
    act_hbm, err_hbm, ker_hbm, ig_hbm, kg_hbm,
    raw, act_v, ker_v, e3, at, at_row, wm, fs, ig_v, gs, hs, r1s, r2s, r3s, fins,
    greet2, greet3, lsem, osem, ssem, hsend, hrecv, s1s, s1r, s2s, s2r, s3s, s3r, s4s, s4r, s5s, s5r,
):
    dp = lax.axis_index("dp")
    dep = lax.axis_index("depth")
    he = lax.axis_index("height")
    core = dp % 2
    y = he * 2 + dp // 2
    x = dep // NZ
    z = dep % NZ
    me = y * NX + x
    n_dep = NX * NZ
    up = (dp, (dep + 1) % n_dep, he)
    down = (dp, (dep + n_dep - 1) % n_dep, he)
    side = (dp, dep, 1 - he)
    up_side = (dp, (dep + 1) % n_dep, 1 - he)
    down_side = (dp, (dep + n_dep - 1) % n_dep, 1 - he)
    sibling = device_of(1 - core, x, y, z)
    plane = []
    for j in (10, 6, 14, 9, 11, 5, 7, 13, 15, 2, 8, 1, 3, 4, 12):
        px, py = (x + j % NX) % NX, (y + j // NX) % NY
        plane.append((py * NX + px, device_of(core, px, py, z)))
    line = []
    for j in (4, 3, 5, 2, 6, 1, 7):
        pz = (z + j) % NZ
        line.append((pz, device_of(core, x, y, pz)))

    barrier = pltpu.get_barrier_semaphore()
    x_near = [device_of(core, (x + j) % NX, y, z) for j in (1, 3)]
    y_near = [device_of(core, x, (y + j) % NY, z) for j in (1, 3)]
    z_near = [device_of(core, x, y, (z + j) % NZ) for j in (1, 7)]
    x_ring = [device_of(core, (x + j) % NX, y, z) for j in (2, 1, 3)]
    z_two = [device_of(core, x, y, (z + j) % NZ) for j in (2, 6)]
    first = [up, down, side] + x_near + y_near + z_near + [sibling]

    def greet(sem, devices):
        for d in devices:
            pl.semaphore_signal(sem, inc=1, device_id=d, device_id_type=MESH)

    load_err = pltpu.make_async_copy(err_hbm.at[0], raw.at[1:5, 1:17], lsem.at[0])
    load_act = pltpu.make_async_copy(act_hbm.at[0], act_v, lsem.at[1])
    load_ker = pltpu.make_async_copy(ker_hbm, ker_v, lsem.at[2])
    load_err.start()
    load_act.start()
    load_ker.start()
    greet(barrier, first)

    def remote(src, dst, send, recv, target):
        return pltpu.make_async_remote_copy(
            src_ref=src, dst_ref=dst, send_sem=send, recv_sem=recv,
            device_id=target, device_id_type=MESH,
        )

    row_src = 15 - 15 * he
    row_dst = 17 * he
    row_in = 17 - 17 * he
    halo = [
        remote(err_hbm.at[0, :, row_src], raw.at[1:5, row_dst], hsend.at[0], hrecv.at[0], side),
        remote(err_hbm.at[0, 3], raw.at[0, 1:17], hsend.at[1], hrecv.at[1], up),
        remote(err_hbm.at[0, 0], raw.at[5, 1:17], hsend.at[2], hrecv.at[2], down),
        remote(err_hbm.at[0, 3, row_src], raw.at[0, row_dst], hsend.at[3], hrecv.at[3], up_side),
        remote(err_hbm.at[0, 0, row_src], raw.at[5, row_dst], hsend.at[4], hrecv.at[4], down_side),
    ]

    for s in range(6):
        e3[s, 0] = jnp.zeros((64, 384), BF16)
        e3[s, 17] = jnp.zeros((64, 384), BF16)
    fs[:, 0:8] = jnp.zeros((16, 8, 128), F32)
    fs[:, 72:80] = jnp.zeros((16, 8, 128), F32)
    for g, (rows, n) in zip(gs, CHUNKS):
        used = len(rows) * 24
        if used < 16 * n:
            g[:, used:] = jnp.zeros((2, 16 * n - used, 8, 128), F32)

    def widen(s):
        fs[:, 8:72] = raw[s, 1:17].astype(F32)
        e3[s, 1:17, :, 0:128] = fs[:, 7:71].astype(BF16)
        e3[s, 1:17, :, 128:256] = raw[s, 1:17]
        e3[s, 1:17, :, 256:384] = fs[:, 9:73].astype(BF16)

    def widen_row(s):
        fs[0, 8:72] = raw[s, row_in].astype(F32)
        e3[s, row_in, :, 0:128] = fs[0, 7:71].astype(BF16)
        e3[s, row_in, :, 128:256] = raw[s, row_in]
        e3[s, row_in, :, 256:384] = fs[0, 9:73].astype(BF16)

    load_act.wait()

    @pl.loop(0, 4)
    def _(d):
        at[d] = act_v[d].reshape(1024, 128).T

    at_row[...] = act_v[:, row_src].reshape(256, 128).T
    pl.semaphore_wait(barrier, len(first))
    for c in halo[:3]:
        c.start()
    greet(greet2, [x_near[1], y_near[1], side] + z_near)
    load_err.wait()

    @pl.loop(1, 5)
    def _(s):
        widen(s)

    def grad_terms(a, pairs, h):
        total = None
        for d, s in pairs:
            term = jnp.dot(
                at[d], e3[s, 2 - h : 18 - h].reshape(1024, 384), preferred_element_type=F32
            )
            total = term if total is None else total + term
        return total

    def put(ch, first, total, add):
        g = gs[ch]
        for j in range(3):
            for c in range(2):
                place = (c, pl.ds(first + (2 - j) * 8, 8))
                part = total[c * 64 : (c + 1) * 64, j * 128 : (j + 1) * 128].reshape(8, 8, 128)
                if add:
                    part = part + g[place]
                g[place] = part

    def s1(ch):
        return remote(gs[ch].at[1 - core], r1s[ch], s1s.at[ch], s1r.at[ch], sibling)

    def s2(ch):
        n = CHUNKS[ch][1]
        return [
            remote(hs[ch].at[pl.ds(p * n, n)], r2s[ch].at[me], s2s.at[ch, p], s2r.at[ch, me], d)
            for p, d in plane
        ]

    def s2_arrive(ch):
        n = CHUNKS[ch][1]
        for p, d in plane:
            remote(
                hs[ch].at[pl.ds(p * n, n)], r2s[ch].at[p], s2s.at[ch, p], s2r.at[ch, p], d
            ).wait_recv()

    def s3(ch):
        return [
            remote(r3s[ch].at[z], r3s[ch].at[z], s3s.at[ch, p], s3r.at[ch, z], d) for p, d in line
        ]

    def s4_part(ch, p):
        n = CHUNKS[ch][1]
        return fins[ch].at[core, pl.ds(p * n, n)]

    def s4(ch):
        return [
            remote(s4_part(ch, me), s4_part(ch, me), s4s.at[ch, p], s4r.at[ch, me], d)
            for p, d in plane
        ]

    def s5(ch):
        return remote(fins[ch].at[core], fins[ch].at[core], s5s.at[ch], s5r.at[ch], sibling)

    def step1(ch):
        s1(ch).start()

    def step2(ch):
        s1(ch).wait()
        hs[ch][...] = gs[ch][core] + r1s[ch][...]
        for c in s2(ch):
            c.start()

    def step3(ch):
        n = CHUNKS[ch][1]
        s2_arrive(ch)
        r2s[ch][me] = hs[ch][pl.ds(me * n, n)]
        total = r2s[ch][0]
        for p in range(1, 16):
            total = total + r2s[ch][p]
        r3s[ch][z] = total
        for c in s3(ch):
            c.start()

    def step4(ch):
        n = CHUNKS[ch][1]
        for c in s2(ch):
            c.wait_send()
        for p, d in line:
            remote(r3s[ch].at[z], r3s[ch].at[p], s3s.at[ch, p], s3r.at[ch, p], d).wait_recv()
        total = r3s[ch][0]
        for p in range(1, NZ):
            total = total + r3s[ch][p]
        fins[ch][core, pl.ds(me * n, n)] = total * (1.0 / 1024.0)
        for c in s4(ch):
            c.start()

    def step5(ch):
        for c in s3(ch):
            c.wait_send()
        for p, d in plane:
            remote(s4_part(ch, me), s4_part(ch, p), s4s.at[ch, p], s4r.at[ch, p], d).wait_recv()
        s5(ch).start()
        for copy in outs(ch, core):
            copy.start()

    def outs(ch, c):
        copies = []
        rows, _ = CHUNKS[ch]
        for a in range(3):
            here = [(i, h) for i, (b, h) in enumerate(rows) if b == a]
            if here:
                i, h = here[0]
                k = len(here)
                copies.append(
                    pltpu.make_async_copy(
                        fins[ch].at[c, i * 24 : (i + k) * 24].reshape(3 * k, 8, 8, 128),
                        kg_hbm.at[pl.ds(a * 9 + h * 3, 3 * k), c],
                        osem.at[ch, a, c],
                    )
                )
        return copies

    def step6(ch):
        for c in s4(ch):
            c.wait_send()
        remote(fins[ch].at[core], fins[ch].at[1 - core], s5s.at[ch], s5r.at[ch], sibling).wait()
        for copy in outs(ch, 1 - core):
            copy.start()

    def build_weights():
        @pl.loop(0, 3)
        def _(a):
            for r in range(4):
                for e in range(2):
                    tap = e + 2 - r
                    for j in range(3):
                        if 0 <= tap <= 2:
                            block = ker_v[a * 9 + tap * 3 + 2 - j].T
                        else:
                            block = jnp.zeros((128, 128), BF16)
                        wm[a * 4 + r, j * 128 : (j + 1) * 128, e * 128 : (e + 1) * 128] = block

    def add_terms(a, h, pairs, add):
        ch, first = PLACE[a, h]
        put(ch, first, grad_terms(a, pairs, h), add)

    for h in range(3):
        add_terms(1, h, [(d, d + 1) for d in range(4)], False)
    pl.semaphore_wait(greet2, 5)
    for c in halo[3:]:
        c.start()
    greet(greet3, x_ring + z_two)
    halo[0].wait()

    @pl.loop(1, 5)
    def _(s):
        widen_row(s)

    beyond = e3[1:5, row_in].reshape(256, 384)
    put(0, he * 48, jnp.dot(at_row[...], beyond, preferred_element_type=F32), True)
    step1(0)
    for h in range(3):
        add_terms(0, h, [(d, d + 2) for d in range(3)], False)
    pl.semaphore_wait(greet3, 5)
    step2(0)
    for h in range(3):
        add_terms(2, h, [(d + 1, d + 1) for d in range(3)], False)

    for i, s in enumerate((5, 0)):
        halo[2 - i].wait()
        halo[4 - i].wait()
        widen(s)
        widen_row(s)

        @pl.when(dep == (n_dep - 1) * (1 - i))
        def _():
            e3[s] = jnp.zeros((18, 64, 384), BF16)

        for h in range(3):
            add_terms(2 * i, h, [(3 - 3 * i, s)], True)
            if (2 * i, h) == CHUNKS[1][0][-1]:
                step1(1)
    step1(2)
    step2(1)
    step2(2)
    step3(0)
    load_ker.wait()
    build_weights()

    @pl.loop(0, 4)
    def _(d):
        acc = jnp.zeros((512, 256), F32)
        for a in range(3):
            rows = e3.at[d + 2 - a]
            for r in range(4):
                part = rows[...].reshape(9, 2, 64, 384)[r // 2 : r // 2 + 8, r % 2]
                acc += jnp.dot(part.reshape(512, 384), wm[a * 4 + r], preferred_element_type=F32)
        for e in range(2):
            half = acc[:, e * 128 : (e + 1) * 128].astype(BF16).reshape(8, 64, 128)
            for k in range(8):
                ig_v[d, 2 * k + e] = half[k]

        @pl.when(d == 2)
        def _():
            step3(1)
            step3(2)
            step4(0)

    store = pltpu.make_async_copy(ig_v, ig_hbm.at[0], ssem)
    store.start()
    step4(1)
    step4(2)
    step5(0)
    step5(1)
    step6(0)
    step5(2)
    step6(1)
    step6(2)
    for ch in range(len(CHUNKS)):
        for c in range(2):
            for copy in outs(ch, c):
                copy.wait()
    store.wait()


def local(activations, error_signal, kernel):
    any_spec = pl.BlockSpec(memory_space=pl.ANY)
    tiles = [n for _, n in CHUNKS]
    count = len(CHUNKS)

    def per_chunk(shape):
        return [pltpu.VMEM(shape(n) + (8, 128), F32) for n in tiles]

    dma = pltpu.SemaphoreType.DMA
    input_grad, packed = pl.pallas_call(
        body,
        out_shape=(
            jax.ShapeDtypeStruct(activations.shape, BF16),
            jax.ShapeDtypeStruct((27, 2, 8, 8, 128), F32),
        ),
        in_specs=[any_spec] * 3,
        out_specs=(any_spec, any_spec),
        scratch_shapes=[
            pltpu.VMEM((6, 18, 64, 128), BF16),
            pltpu.VMEM((4, 16, 64, 128), BF16),
            pltpu.VMEM((27, 128, 128), BF16),
            pltpu.VMEM((6, 18, 64, 384), BF16),
            pltpu.VMEM((4, 128, 1024), BF16),
            pltpu.VMEM((128, 256), BF16),
            pltpu.VMEM((12, 384, 256), BF16),
            pltpu.VMEM((16, 80, 128), F32),
            pltpu.VMEM((4, 16, 64, 128), BF16),
            per_chunk(lambda n: (2, 16 * n)),
            per_chunk(lambda n: (16 * n,)),
            per_chunk(lambda n: (16 * n,)),
            per_chunk(lambda n: (16, n)),
            per_chunk(lambda n: (NZ, n)),
            per_chunk(lambda n: (2, 16 * n)),
            pltpu.SemaphoreType.REGULAR,
            pltpu.SemaphoreType.REGULAR,
            dma((3,)),
            dma((count, 3, 2)),
            dma,
            dma((5,)),
            dma((5,)),
            dma((count,)),
            dma((count,)),
            dma((count, 16)),
            dma((count, 16)),
            dma((count, NZ)),
            dma((count, NZ)),
            dma((count, 16)),
            dma((count, 16)),
            dma((count,)),
            dma((count,)),
        ],
        compiler_params=pltpu.CompilerParams(
            collective_id=0, has_side_effects=True, vmem_limit_bytes=60 << 20
        ),
        cost_estimate=pl.CostEstimate(flops=8 << 30, bytes_accessed=6 << 20, transcendentals=0),
        name="conv_grads",
    )(activations, error_signal, kernel.reshape(27, 128, 128))
    return (input_grad, packed.reshape(3, 3, 3, 128, 128))


def solution(mesh):
    placed = P("dp", "depth", "height", None, None)
    return jax.shard_map(
        local,
        mesh=mesh,
        in_specs=(placed, placed, P()),
        out_specs=(placed, P()),
        check_vma=False,
    )
```

```python
import functools

import jax
import jax.numpy as jnp
from jax import lax
from jax.experimental import pallas as pl
from jax.experimental.pallas import tpu as pltpu
from jax.sharding import PartitionSpec as P

MESH = pl.DeviceIdType.MESH
F32 = jnp.float32
BF16 = jnp.bfloat16
NX, NY, NZ = 4, 4, 8
CHUNKS = (
    (((1, 0), (1, 1), (1, 2)), 5),
    (((0, 0), (0, 1), (0, 2), (2, 0)), 6),
    (((2, 1), (2, 2)), 3),
)
PLACE = {row: (ch, 24 * i) for ch, (rows, _) in enumerate(CHUNKS) for i, row in enumerate(rows)}


def device_of(core, x, y, z):
    return ((y % 2) * 2 + core, x * NZ + z, y // 2)


def body(
    act_hbm, err_hbm, ker_hbm, ig_hbm, kg_hbm,
    raw, act_v, ker_v, e3, at, at_row, wm, fs, ig_v, gs, hs, r1s, r2s, r3s, fins,
    greet2, greet3, lsem, osem, ssem, hsend, hrecv, s1s, s1r, s2s, s2r, s3s, s3r, s4s, s4r, s5s, s5r,
):
    dp = lax.axis_index("dp")
    dep = lax.axis_index("depth")
    he = lax.axis_index("height")
    core = dp % 2
    y = he * 2 + dp // 2
    x = dep // NZ
    z = dep % NZ
    me = y * NX + x
    n_dep = NX * NZ
    up = (dp, (dep + 1) % n_dep, he)
    down = (dp, (dep + n_dep - 1) % n_dep, he)
    side = (dp, dep, 1 - he)
    up_side = (dp, (dep + 1) % n_dep, 1 - he)
    down_side = (dp, (dep + n_dep - 1) % n_dep, 1 - he)
    sibling = device_of(1 - core, x, y, z)
    plane = []
    for j in (10, 6, 14, 9, 11, 5, 7, 13, 15, 2, 8, 1, 3, 4, 12):
        px, py = (x + j % NX) % NX, (y + j // NX) % NY
        plane.append((py * NX + px, device_of(core, px, py, z)))
    line = []
    for j in (4, 3, 5, 2, 6, 1, 7):
        pz = (z + j) % NZ
        line.append((pz, device_of(core, x, y, pz)))

    barrier = pltpu.get_barrier_semaphore()
    x_near = [device_of(core, (x + j) % NX, y, z) for j in (1, 3)]
    y_near = [device_of(core, x, (y + j) % NY, z) for j in (1, 3)]
    z_near = [device_of(core, x, y, (z + j) % NZ) for j in (1, 7)]
    x_ring = [device_of(core, (x + j) % NX, y, z) for j in (2, 1, 3)]
    z_two = [device_of(core, x, y, (z + j) % NZ) for j in (2, 6)]
    first = [up, down, side] + x_near + y_near + z_near + [sibling]

    def greet(sem, devices):
        for d in devices:
            pl.semaphore_signal(sem, inc=1, device_id=d, device_id_type=MESH)

    load_err = pltpu.make_async_copy(err_hbm.at[0], raw.at[1:5, 1:17], lsem.at[0])
    load_act = pltpu.make_async_copy(act_hbm.at[0], act_v, lsem.at[1])
    load_ker = pltpu.make_async_copy(ker_hbm, ker_v, lsem.at[2])
    load_err.start()
    load_act.start()
    load_ker.start()
    greet(barrier, first)

    def remote(src, dst, send, recv, target):
        return pltpu.make_async_remote_copy(
            src_ref=src, dst_ref=dst, send_sem=send, recv_sem=recv,
            device_id=target, device_id_type=MESH,
        )

    row_src = 15 - 15 * he
    row_dst = 17 * he
    row_in = 17 - 17 * he
    halo = [
        remote(raw.at[1:5, row_src + 1], raw.at[1:5, row_dst], hsend.at[0], hrecv.at[0], side),
        remote(raw.at[4, 1:17], raw.at[0, 1:17], hsend.at[1], hrecv.at[1], up),
        remote(raw.at[1, 1:17], raw.at[5, 1:17], hsend.at[2], hrecv.at[2], down),
        remote(raw.at[4, row_src + 1], raw.at[0, row_dst], hsend.at[3], hrecv.at[3], up_side),
        remote(raw.at[1, row_src + 1], raw.at[5, row_dst], hsend.at[4], hrecv.at[4], down_side),
    ]

    for s in range(6):
        e3[s, 0] = jnp.zeros((64, 384), BF16)
        e3[s, 17] = jnp.zeros((64, 384), BF16)
    fs[:, 0:8] = jnp.zeros((16, 8, 128), F32)
    fs[:, 72:80] = jnp.zeros((16, 8, 128), F32)
    for g, (rows, n) in zip(gs, CHUNKS):
        used = len(rows) * 24
        if used < 16 * n:
            g[:, used:] = jnp.zeros((2, 16 * n - used, 8, 128), F32)

    def widen(s):
        fs[:, 8:72] = raw[s, 1:17].astype(F32)
        e3[s, 1:17, :, 0:128] = fs[:, 7:71].astype(BF16)
        e3[s, 1:17, :, 128:256] = raw[s, 1:17]
        e3[s, 1:17, :, 256:384] = fs[:, 9:73].astype(BF16)

    def widen_row(s):
        fs[0, 8:72] = raw[s, row_in].astype(F32)
        e3[s, row_in, :, 0:128] = fs[0, 7:71].astype(BF16)
        e3[s, row_in, :, 128:256] = raw[s, row_in]
        e3[s, row_in, :, 256:384] = fs[0, 9:73].astype(BF16)

    load_act.wait()

    @pl.loop(0, 4)
    def _(d):
        at[d] = act_v[d].reshape(1024, 128).T

    at_row[...] = act_v[:, row_src].reshape(256, 128).T
    load_err.wait()
    pl.semaphore_wait(barrier, len(first))
    for c in halo[:3]:
        c.start()
    greet(greet2, [x_near[1], y_near[1], side] + z_near)

    @pl.loop(1, 5)
    def _(s):
        widen(s)

    def grad_terms(a, pairs, h):
        total = None
        for d, s in pairs:
            term = jnp.dot(
                at[d], e3[s, 2 - h : 18 - h].reshape(1024, 384), preferred_element_type=F32
            )
            total = term if total is None else total + term
        return total

    def put(ch, first, total, add):
        g = gs[ch]
        for j in range(3):
            for c in range(2):
                place = (c, pl.ds(first + (2 - j) * 8, 8))
                part = total[c * 64 : (c + 1) * 64, j * 128 : (j + 1) * 128].reshape(8, 8, 128)
                if add:
                    part = part + g[place]
                g[place] = part

    def s1(ch):
        return remote(gs[ch].at[1 - core], r1s[ch], s1s.at[ch], s1r.at[ch], sibling)

    def s2(ch):
        n = CHUNKS[ch][1]
        return [
            remote(hs[ch].at[pl.ds(p * n, n)], r2s[ch].at[me], s2s.at[ch, p], s2r.at[ch, me], d)
            for p, d in plane
        ]

    def s2_arrive(ch):
        n = CHUNKS[ch][1]
        for p, d in plane:
            remote(
                hs[ch].at[pl.ds(p * n, n)], r2s[ch].at[p], s2s.at[ch, p], s2r.at[ch, p], d
            ).wait_recv()

    def s3(ch):
        return [
            remote(r3s[ch].at[z], r3s[ch].at[z], s3s.at[ch, p], s3r.at[ch, z], d) for p, d in line
        ]

    def s4_part(ch, p):
        n = CHUNKS[ch][1]
        return fins[ch].at[core, pl.ds(p * n, n)]

    def s4(ch):
        return [
            remote(s4_part(ch, me), s4_part(ch, me), s4s.at[ch, p], s4r.at[ch, me], d)
            for p, d in plane
        ]

    def taps_of(ch):
        rows, _ = CHUNKS[ch]
        runs = []
        for a in range(3):
            here = [(i, h) for i, (b, h) in enumerate(rows) if b == a]
            if here:
                i, h = here[0]
                runs.append((i * 24, len(here) * 3, a * 9 + h * 3))
        return runs

    def half(ch, c, run):
        first, k, tap = run
        return (
            fins[ch].at[c, first : first + 8 * k].reshape(k, 8, 8, 128),
            kg_hbm.at[tap : tap + k, c],
        )

    def s5(ch, c):
        copies = []
        for i, run in enumerate(taps_of(ch)):
            src, dst = half(ch, c, run)
            copies.append(remote(src, dst, s5s.at[ch, i], s5r.at[ch, i], sibling))
        return copies

    def outs(ch):
        copies = []
        for i, run in enumerate(taps_of(ch)):
            src, dst = half(ch, core, run)
            copies.append(pltpu.make_async_copy(src, dst, osem.at[ch, i]))
        return copies

    def step1(ch):
        s1(ch).start()

    def step2(ch):
        n = CHUNKS[ch][1]
        s1(ch).wait()
        for (p, _), c in zip(plane, s2(ch)):
            piece = pl.ds(p * n, n)
            hs[ch][piece] = gs[ch][core, piece] + r1s[ch][piece]
            c.start()
        mine = pl.ds(me * n, n)
        r2s[ch][me] = gs[ch][core, mine] + r1s[ch][mine]

    def step3(ch):
        n = CHUNKS[ch][1]
        s2_arrive(ch)
        total = r2s[ch][0]
        for p in range(1, 16):
            total = total + r2s[ch][p]
        r3s[ch][z] = total
        for c in s3(ch):
            c.start()

    def step4(ch):
        n = CHUNKS[ch][1]
        for c in s2(ch):
            c.wait_send()
        for p, d in line:
            remote(r3s[ch].at[z], r3s[ch].at[p], s3s.at[ch, p], s3r.at[ch, p], d).wait_recv()
        total = r3s[ch][0]
        for p in range(1, NZ):
            total = total + r3s[ch][p]
        fins[ch][core, pl.ds(me * n, n)] = total * (1.0 / 1024.0)
        for c in s4(ch):
            c.start()

    def step5(ch):
        for c in s3(ch):
            c.wait_send()
        for p, d in plane:
            remote(s4_part(ch, me), s4_part(ch, p), s4s.at[ch, p], s4r.at[ch, p], d).wait_recv()
        for c in s5(ch, core) + outs(ch):
            c.start()

    def step6(ch):
        for c in s4(ch):
            c.wait_send()
        for c in s5(ch, core):
            c.wait_send()
        for c in s5(ch, 1 - core):
            c.wait_recv()
        for c in outs(ch):
            c.wait()

    def build_weights():
        @pl.loop(0, 3)
        def _(a):
            for r in range(4):
                for e in range(2):
                    tap = e + 2 - r
                    for j in range(3):
                        if 0 <= tap <= 2:
                            block = ker_v[a * 9 + tap * 3 + 2 - j].T
                        else:
                            block = jnp.zeros((128, 128), BF16)
                        wm[a * 4 + r, j * 128 : (j + 1) * 128, e * 128 : (e + 1) * 128] = block

    def add_terms(a, h, pairs, add):
        ch, first = PLACE[a, h]
        put(ch, first, grad_terms(a, pairs, h), add)

    for h in range(3):
        add_terms(1, h, [(d, d + 1) for d in range(4)], False)
    pl.semaphore_wait(greet2, 5)
    for c in halo[3:]:
        c.start()
    greet(greet3, x_ring + z_two)
    halo[0].wait()

    @pl.loop(1, 5)
    def _(s):
        widen_row(s)

    beyond = e3[1:5, row_in].reshape(256, 384)
    put(0, he * 48, jnp.dot(at_row[...], beyond, preferred_element_type=F32), True)
    step1(0)
    for h in range(3):
        add_terms(0, h, [(d, d + 2) for d in range(3)], False)
    pl.semaphore_wait(greet3, 5)
    step2(0)
    for h in range(3):
        add_terms(2, h, [(d + 1, d + 1) for d in range(3)], False)

    for i, s in enumerate((5, 0)):
        halo[2 - i].wait()
        halo[4 - i].wait()
        widen(s)
        widen_row(s)

        @pl.when(dep == (n_dep - 1) * (1 - i))
        def _():
            e3[s] = jnp.zeros((18, 64, 384), BF16)

        for h in range(3):
            add_terms(2 * i, h, [(3 - 3 * i, s)], True)
            if (2 * i, h) == CHUNKS[1][0][-1]:
                step1(1)
    step1(2)
    step2(1)
    step2(2)
    step3(0)
    load_ker.wait()
    build_weights()

    @pl.loop(0, 4)
    def _(d):
        acc = jnp.zeros((512, 256), F32)
        for a in range(3):
            rows = e3.at[d + 2 - a]
            for r in range(4):
                part = rows[...].reshape(9, 2, 64, 384)[r // 2 : r // 2 + 8, r % 2]
                acc += jnp.dot(part.reshape(512, 384), wm[a * 4 + r], preferred_element_type=F32)
        for e in range(2):
            half = acc[:, e * 128 : (e + 1) * 128].astype(BF16).reshape(8, 64, 128)
            for k in range(8):
                ig_v[d, 2 * k + e] = half[k]

        @pl.when(d == 2)
        def _():
            step3(1)
            step3(2)
            step4(0)

    store = pltpu.make_async_copy(ig_v, ig_hbm.at[0], ssem)
    store.start()
    step4(1)
    step4(2)
    step5(0)
    step5(1)
    step6(0)
    step5(2)
    step6(1)
    step6(2)
    store.wait()


def local(activations, error_signal, kernel):
    any_spec = pl.BlockSpec(memory_space=pl.ANY)
    tiles = [n for _, n in CHUNKS]
    count = len(CHUNKS)

    def per_chunk(shape):
        return [pltpu.VMEM(shape(n) + (8, 128), F32) for n in tiles]

    dma = pltpu.SemaphoreType.DMA
    input_grad, packed = pl.pallas_call(
        body,
        out_shape=(
            jax.ShapeDtypeStruct(activations.shape, BF16),
            jax.ShapeDtypeStruct((27, 2, 8, 8, 128), F32),
        ),
        in_specs=[any_spec] * 3,
        out_specs=(any_spec, any_spec),
        scratch_shapes=[
            pltpu.VMEM((6, 18, 64, 128), BF16),
            pltpu.VMEM((4, 16, 64, 128), BF16),
            pltpu.VMEM((27, 128, 128), BF16),
            pltpu.VMEM((6, 18, 64, 384), BF16),
            pltpu.VMEM((4, 128, 1024), BF16),
            pltpu.VMEM((128, 256), BF16),
            pltpu.VMEM((12, 384, 256), BF16),
            pltpu.VMEM((16, 80, 128), F32),
            pltpu.VMEM((4, 16, 64, 128), BF16),
            per_chunk(lambda n: (2, 16 * n)),
            per_chunk(lambda n: (16 * n,)),
            per_chunk(lambda n: (16 * n,)),
            per_chunk(lambda n: (16, n)),
            per_chunk(lambda n: (NZ, n)),
            per_chunk(lambda n: (2, 16 * n)),
            pltpu.SemaphoreType.REGULAR,
            pltpu.SemaphoreType.REGULAR,
            dma((3,)),
            dma((count, 3)),
            dma,
            dma((5,)),
            dma((5,)),
            dma((count,)),
            dma((count,)),
            dma((count, 16)),
            dma((count, 16)),
            dma((count, NZ)),
            dma((count, NZ)),
            dma((count, 16)),
            dma((count, 16)),
            dma((count, 3)),
            dma((count, 3)),
        ],
        compiler_params=pltpu.CompilerParams(
            collective_id=0, has_side_effects=True, vmem_limit_bytes=60 << 20
        ),
        cost_estimate=pl.CostEstimate(flops=8 << 30, bytes_accessed=6 << 20, transcendentals=0),
        name="conv_grads",
    )(activations, error_signal, kernel.reshape(27, 128, 128))
    return finish(input_grad, packed.reshape(3, 3, 3, 128, 128))


def finish_body(ig_in, kg_in, ig_out, kg_out, ig_v, kg_v, sems):
    moves = [(kg_in.at[i], kg_v.at[i], kg_out.at[i]) for i in range(3)]
    moves += [(ig_in.at[0, i], ig_v.at[i], ig_out.at[0, i]) for i in range(4)]
    loads = [pltpu.make_async_copy(a, b, sems.at[0, i]) for i, (a, b, _) in enumerate(moves)]
    stores = [pltpu.make_async_copy(b, c, sems.at[1, i]) for i, (_, b, c) in enumerate(moves)]
    for c in loads:
        c.start()
    for load, store in zip(loads, stores):
        load.wait()
        store.start()
    for c in stores:
        c.wait()


def finish(ig, kg):
    any_spec = pl.BlockSpec(memory_space=pl.ANY)
    return pl.pallas_call(
        finish_body,
        out_shape=(jax.ShapeDtypeStruct(ig.shape, BF16), jax.ShapeDtypeStruct(kg.shape, F32)),
        in_specs=[any_spec] * 2,
        out_specs=(any_spec, any_spec),
        scratch_shapes=[
            pltpu.VMEM(ig.shape[1:], BF16),
            pltpu.VMEM(kg.shape, F32),
            pltpu.SemaphoreType.DMA((2, 7)),
        ],
        compiler_params=pltpu.CompilerParams(vmem_limit_bytes=60 << 20),
        name="finish",
    )(ig, kg)


def solution(mesh):
    placed = P("dp", "depth", "height", None, None)
    return jax.shard_map(
        local,
        mesh=mesh,
        in_specs=(placed, placed, P()),
        out_specs=(placed, P()),
        check_vma=False,
    )
```

```python
import functools

import jax
import jax.numpy as jnp
from jax import lax
from jax.experimental import pallas as pl
from jax.experimental.pallas import tpu as pltpu
from jax.sharding import PartitionSpec as P

MESH = pl.DeviceIdType.MESH
F32 = jnp.float32
BF16 = jnp.bfloat16
NX, NY, NZ = 4, 4, 8
CHUNKS = (
    (((1, 0), (1, 1), (1, 2)), 5),
    (((0, 0), (0, 1)), 3),
    (((0, 2), (2, 0)), 3),
    (((2, 1), (2, 2)), 3),
)
PLACE = {row: (ch, 24 * i) for ch, (rows, _) in enumerate(CHUNKS) for i, row in enumerate(rows)}


def device_of(core, x, y, z):
    return ((y % 2) * 2 + core, x * NZ + z, y // 2)


def body(
    act_hbm, err_hbm, ker_hbm, ig_hbm, kg_hbm,
    raw, act_v, ker_v, e3, at, at_row, wm, fs, ig_v, gs, hs, r1s, r2s, r3s, fins,
    greet2, greet3, lsem, osem, ssem, hsend, hrecv, s1s, s1r, s2s, s2r, s3s, s3r, s4s, s4r, s5s, s5r,
):
    dp = lax.axis_index("dp")
    dep = lax.axis_index("depth")
    he = lax.axis_index("height")
    core = dp % 2
    y = he * 2 + dp // 2
    x = dep // NZ
    z = dep % NZ
    me = y * NX + x
    n_dep = NX * NZ
    up = (dp, (dep + 1) % n_dep, he)
    down = (dp, (dep + n_dep - 1) % n_dep, he)
    side = (dp, dep, 1 - he)
    up_side = (dp, (dep + 1) % n_dep, 1 - he)
    down_side = (dp, (dep + n_dep - 1) % n_dep, 1 - he)
    sibling = device_of(1 - core, x, y, z)
    plane = []
    for j in (10, 6, 14, 9, 11, 5, 7, 13, 15, 2, 8, 1, 3, 4, 12):
        px, py = (x + j % NX) % NX, (y + j // NX) % NY
        plane.append((py * NX + px, device_of(core, px, py, z)))
    line = []
    for j in (4, 3, 5, 2, 6, 1, 7):
        pz = (z + j) % NZ
        line.append((pz, device_of(core, x, y, pz)))

    barrier = pltpu.get_barrier_semaphore()
    x_near = [device_of(core, (x + j) % NX, y, z) for j in (1, 3)]
    y_near = [device_of(core, x, (y + j) % NY, z) for j in (1, 3)]
    z_near = [device_of(core, x, y, (z + j) % NZ) for j in (1, 7)]
    x_ring = [device_of(core, (x + j) % NX, y, z) for j in (2, 1, 3)]
    z_two = [device_of(core, x, y, (z + j) % NZ) for j in (2, 6)]
    first = [up, down, side] + x_near + y_near + z_near + [sibling]

    def greet(sem, devices):
        for d in devices:
            pl.semaphore_signal(sem, inc=1, device_id=d, device_id_type=MESH)

    load_err = pltpu.make_async_copy(err_hbm.at[0], raw.at[1:5, 1:17], lsem.at[0])
    load_act = pltpu.make_async_copy(act_hbm.at[0], act_v, lsem.at[1])
    load_ker = pltpu.make_async_copy(ker_hbm, ker_v, lsem.at[2])
    load_err.start()
    load_act.start()
    load_ker.start()
    greet(barrier, first)

    def remote(src, dst, send, recv, target):
        return pltpu.make_async_remote_copy(
            src_ref=src, dst_ref=dst, send_sem=send, recv_sem=recv,
            device_id=target, device_id_type=MESH,
        )

    row_src = 15 - 15 * he
    row_dst = 17 * he
    row_in = 17 - 17 * he
    halo = [
        remote(raw.at[1:5, row_src + 1], raw.at[1:5, row_dst], hsend.at[0], hrecv.at[0], side),
        remote(raw.at[4, 1:17], raw.at[0, 1:17], hsend.at[1], hrecv.at[1], up),
        remote(raw.at[1, 1:17], raw.at[5, 1:17], hsend.at[2], hrecv.at[2], down),
        remote(raw.at[4, row_src + 1], raw.at[0, row_dst], hsend.at[3], hrecv.at[3], up_side),
        remote(raw.at[1, row_src + 1], raw.at[5, row_dst], hsend.at[4], hrecv.at[4], down_side),
    ]

    for s in range(6):
        e3[s, 0] = jnp.zeros((64, 384), BF16)
        e3[s, 17] = jnp.zeros((64, 384), BF16)
    fs[:, 0:8] = jnp.zeros((16, 8, 128), F32)
    fs[:, 72:80] = jnp.zeros((16, 8, 128), F32)
    for g, (rows, n) in zip(gs, CHUNKS):
        used = len(rows) * 24
        if used < 16 * n:
            g[:, used:] = jnp.zeros((2, 16 * n - used, 8, 128), F32)

    def widen(s):
        fs[:, 8:72] = raw[s, 1:17].astype(F32)
        e3[s, 1:17, :, 0:128] = fs[:, 7:71].astype(BF16)
        e3[s, 1:17, :, 128:256] = raw[s, 1:17]
        e3[s, 1:17, :, 256:384] = fs[:, 9:73].astype(BF16)

    def widen_row(s):
        fs[0, 8:72] = raw[s, row_in].astype(F32)
        e3[s, row_in, :, 0:128] = fs[0, 7:71].astype(BF16)
        e3[s, row_in, :, 128:256] = raw[s, row_in]
        e3[s, row_in, :, 256:384] = fs[0, 9:73].astype(BF16)

    load_act.wait()

    @pl.loop(0, 4)
    def _(d):
        at[d] = act_v[d].reshape(1024, 128).T

    at_row[...] = act_v[:, row_src].reshape(256, 128).T
    load_err.wait()
    pl.semaphore_wait(barrier, len(first))
    for c in halo[:3]:
        c.start()
    greet(greet2, [x_near[1], y_near[1], side] + z_near)

    @pl.loop(1, 5)
    def _(s):
        widen(s)

    def grad_terms(a, pairs, h):
        total = None
        for d, s in pairs:
            term = jnp.dot(
                at[d], e3[s, 2 - h : 18 - h].reshape(1024, 384), preferred_element_type=F32
            )
            total = term if total is None else total + term
        return total

    def put(ch, first, total, add):
        g = gs[ch]
        for j in range(3):
            for c in range(2):
                place = (c, pl.ds(first + (2 - j) * 8, 8))
                part = total[c * 64 : (c + 1) * 64, j * 128 : (j + 1) * 128].reshape(8, 8, 128)
                if add:
                    part = part + g[place]
                g[place] = part

    def s1(ch):
        return remote(gs[ch].at[1 - core], r1s[ch], s1s.at[ch], s1r.at[ch], sibling)

    def s2(ch):
        n = CHUNKS[ch][1]
        return [
            remote(hs[ch].at[pl.ds(p * n, n)], r2s[ch].at[me], s2s.at[ch, p], s2r.at[ch, me], d)
            for p, d in plane
        ]

    def s2_arrive(ch):
        n = CHUNKS[ch][1]
        for p, d in plane:
            remote(
                hs[ch].at[pl.ds(p * n, n)], r2s[ch].at[p], s2s.at[ch, p], s2r.at[ch, p], d
            ).wait_recv()

    def s3(ch):
        return [
            remote(r3s[ch].at[z], r3s[ch].at[z], s3s.at[ch, p], s3r.at[ch, z], d) for p, d in line
        ]

    def s4_part(ch, p):
        n = CHUNKS[ch][1]
        return fins[ch].at[core, pl.ds(p * n, n)]

    def s4(ch):
        return [
            remote(s4_part(ch, me), s4_part(ch, me), s4s.at[ch, p], s4r.at[ch, me], d)
            for p, d in plane
        ]

    def taps_of(ch):
        rows, _ = CHUNKS[ch]
        runs = []
        for a in range(3):
            here = [(i, h) for i, (b, h) in enumerate(rows) if b == a]
            if here:
                i, h = here[0]
                runs.append((i * 24, len(here) * 3, a * 9 + h * 3))
        return runs

    def half(ch, c, run):
        first, k, tap = run
        return (
            fins[ch].at[c, first : first + 8 * k].reshape(k, 8, 8, 128),
            kg_hbm.at[tap : tap + k, c],
        )

    def s5(ch, c):
        copies = []
        for i, run in enumerate(taps_of(ch)):
            src, dst = half(ch, c, run)
            copies.append(remote(src, dst, s5s.at[ch, i], s5r.at[ch, i], sibling))
        return copies

    def outs(ch):
        copies = []
        for i, run in enumerate(taps_of(ch)):
            src, dst = half(ch, core, run)
            copies.append(pltpu.make_async_copy(src, dst, osem.at[ch, i]))
        return copies

    def step1(ch):
        s1(ch).start()

    def step2(ch):
        n = CHUNKS[ch][1]
        s1(ch).wait()
        for (p, _), c in zip(plane, s2(ch)):
            piece = pl.ds(p * n, n)
            hs[ch][piece] = gs[ch][core, piece] + r1s[ch][piece]
            c.start()
        mine = pl.ds(me * n, n)
        r2s[ch][me] = gs[ch][core, mine] + r1s[ch][mine]

    def step3(ch):
        n = CHUNKS[ch][1]
        s2_arrive(ch)
        total = r2s[ch][0]
        for p in range(1, 16):
            total = total + r2s[ch][p]
        r3s[ch][z] = total
        for c in s3(ch):
            c.start()

    def step4(ch):
        n = CHUNKS[ch][1]
        for c in s2(ch):
            c.wait_send()
        for p, d in line:
            remote(r3s[ch].at[z], r3s[ch].at[p], s3s.at[ch, p], s3r.at[ch, p], d).wait_recv()
        total = r3s[ch][0]
        for p in range(1, NZ):
            total = total + r3s[ch][p]
        fins[ch][core, pl.ds(me * n, n)] = total * (1.0 / 1024.0)
        for c in s4(ch):
            c.start()

    def step5(ch):
        for c in s3(ch):
            c.wait_send()
        for p, d in plane:
            remote(s4_part(ch, me), s4_part(ch, p), s4s.at[ch, p], s4r.at[ch, p], d).wait_recv()
        for c in s5(ch, core) + outs(ch):
            c.start()

    def step6(ch):
        for c in s4(ch):
            c.wait_send()
        for c in s5(ch, core):
            c.wait_send()
        for c in s5(ch, 1 - core):
            c.wait_recv()
        for c in outs(ch):
            c.wait()

    def build_weights():
        @pl.loop(0, 3)
        def _(a):
            for r in range(4):
                for e in range(2):
                    tap = e + 2 - r
                    for j in range(3):
                        if 0 <= tap <= 2:
                            block = ker_v[a * 9 + tap * 3 + 2 - j].T
                        else:
                            block = jnp.zeros((128, 128), BF16)
                        wm[a * 4 + r, j * 128 : (j + 1) * 128, e * 128 : (e + 1) * 128] = block

    def add_terms(a, h, pairs, add):
        ch, first = PLACE[a, h]
        put(ch, first, grad_terms(a, pairs, h), add)

    for h in range(3):
        add_terms(1, h, [(d, d + 1) for d in range(4)], False)
    pl.semaphore_wait(greet2, 5)
    for c in halo[3:]:
        c.start()
    greet(greet3, x_ring + z_two)
    halo[0].wait()

    @pl.loop(1, 5)
    def _(s):
        widen_row(s)

    beyond = e3[1:5, row_in].reshape(256, 384)
    put(0, he * 48, jnp.dot(at_row[...], beyond, preferred_element_type=F32), True)
    step1(0)
    for h in range(3):
        add_terms(0, h, [(d, d + 2) for d in range(3)], False)
    pl.semaphore_wait(greet3, 5)
    step2(0)
    for h in range(3):
        add_terms(2, h, [(d + 1, d + 1) for d in range(3)], False)

    for i, s in enumerate((5, 0)):
        halo[2 - i].wait()
        halo[4 - i].wait()
        widen(s)
        widen_row(s)

        @pl.when(dep == (n_dep - 1) * (1 - i))
        def _():
            e3[s] = jnp.zeros((18, 64, 384), BF16)

        for h in range(3):
            add_terms(2 * i, h, [(3 - 3 * i, s)], True)
            ch, _ = PLACE[2 * i, h]
            if (2 * i, h) == CHUNKS[ch][0][-1]:
                step1(ch)
                if ch > 1:
                    step2(ch - 1)
    step2(3)
    step3(0)
    load_ker.wait()
    build_weights()

    @pl.loop(0, 4)
    def _(d):
        acc = jnp.zeros((512, 256), F32)
        for a in range(3):
            rows = e3.at[d + 2 - a]
            for r in range(4):
                part = rows[...].reshape(9, 2, 64, 384)[r // 2 : r // 2 + 8, r % 2]
                acc += jnp.dot(part.reshape(512, 384), wm[a * 4 + r], preferred_element_type=F32)
        for e in range(2):
            half = acc[:, e * 128 : (e + 1) * 128].astype(BF16).reshape(8, 64, 128)
            for k in range(8):
                ig_v[d, 2 * k + e] = half[k]

        @pl.when(d == 1)
        def _():
            step3(1)

        @pl.when(d == 2)
        def _():
            step3(2)
            step3(3)
            step4(0)

    store = pltpu.make_async_copy(ig_v, ig_hbm.at[0], ssem)
    store.start()
    step4(1)
    step4(2)
    step4(3)
    step5(0)
    step5(1)
    step6(0)
    step5(2)
    step5(3)
    step6(1)
    step6(2)
    step6(3)
    store.wait()


def local(activations, error_signal, kernel):
    any_spec = pl.BlockSpec(memory_space=pl.ANY)
    tiles = [n for _, n in CHUNKS]
    count = len(CHUNKS)

    def per_chunk(shape):
        return [pltpu.VMEM(shape(n) + (8, 128), F32) for n in tiles]

    dma = pltpu.SemaphoreType.DMA
    input_grad, packed = pl.pallas_call(
        body,
        out_shape=(
            jax.ShapeDtypeStruct(activations.shape, BF16),
            jax.ShapeDtypeStruct((27, 2, 8, 8, 128), F32),
        ),
        in_specs=[any_spec] * 3,
        out_specs=(any_spec, any_spec),
        scratch_shapes=[
            pltpu.VMEM((6, 18, 64, 128), BF16),
            pltpu.VMEM((4, 16, 64, 128), BF16),
            pltpu.VMEM((27, 128, 128), BF16),
            pltpu.VMEM((6, 18, 64, 384), BF16),
            pltpu.VMEM((4, 128, 1024), BF16),
            pltpu.VMEM((128, 256), BF16),
            pltpu.VMEM((12, 384, 256), BF16),
            pltpu.VMEM((16, 80, 128), F32),
            pltpu.VMEM((4, 16, 64, 128), BF16),
            per_chunk(lambda n: (2, 16 * n)),
            per_chunk(lambda n: (16 * n,)),
            per_chunk(lambda n: (16 * n,)),
            per_chunk(lambda n: (16, n)),
            per_chunk(lambda n: (NZ, n)),
            per_chunk(lambda n: (2, 16 * n)),
            pltpu.SemaphoreType.REGULAR,
            pltpu.SemaphoreType.REGULAR,
            dma((3,)),
            dma((count, 3)),
            dma,
            dma((5,)),
            dma((5,)),
            dma((count,)),
            dma((count,)),
            dma((count, 16)),
            dma((count, 16)),
            dma((count, NZ)),
            dma((count, NZ)),
            dma((count, 16)),
            dma((count, 16)),
            dma((count, 3)),
            dma((count, 3)),
        ],
        compiler_params=pltpu.CompilerParams(
            collective_id=0, has_side_effects=True, vmem_limit_bytes=60 << 20
        ),
        cost_estimate=pl.CostEstimate(flops=8 << 30, bytes_accessed=6 << 20, transcendentals=0),
        name="conv_grads",
    )(activations, error_signal, kernel.reshape(27, 128, 128))
    return finish(input_grad, packed.reshape(3, 3, 3, 128, 128))


def finish_body(ig_in, kg_in, ig_out, kg_out, ig_v, kg_v, sems):
    moves = [(kg_in.at[i], kg_v.at[i], kg_out.at[i]) for i in range(3)]
    moves += [(ig_in.at[0, i], ig_v.at[i], ig_out.at[0, i]) for i in range(4)]
    loads = [pltpu.make_async_copy(a, b, sems.at[0, i]) for i, (a, b, _) in enumerate(moves)]
    stores = [pltpu.make_async_copy(b, c, sems.at[1, i]) for i, (_, b, c) in enumerate(moves)]
    for c in loads:
        c.start()
    for load, store in zip(loads, stores):
        load.wait()
        store.start()
    for c in stores:
        c.wait()


def finish(ig, kg):
    any_spec = pl.BlockSpec(memory_space=pl.ANY)
    return pl.pallas_call(
        finish_body,
        out_shape=(jax.ShapeDtypeStruct(ig.shape, BF16), jax.ShapeDtypeStruct(kg.shape, F32)),
        in_specs=[any_spec] * 2,
        out_specs=(any_spec, any_spec),
        scratch_shapes=[
            pltpu.VMEM(ig.shape[1:], BF16),
            pltpu.VMEM(kg.shape, F32),
            pltpu.SemaphoreType.DMA((2, 7)),
        ],
        compiler_params=pltpu.CompilerParams(vmem_limit_bytes=60 << 20),
        name="finish",
    )(ig, kg)


def solution(mesh):
    placed = P("dp", "depth", "height", None, None)
    return jax.shard_map(
        local,
        mesh=mesh,
        in_specs=(placed, placed, P()),
        out_specs=(placed, P()),
        check_vma=False,
    )
```
